512 devices in a mesh: dp: 64 (over z_lo, y, core), mp: 8 (over x, z_hi).
Axes of the slice: x: 4, y: 4, z: 16 (z_hi: 2, z_lo: 8; z = z_hi * 8 + z_lo), core: 2. Of those that a mesh axis runs over, the one named last changes fastest.
Arguments:
- hidden: bfloat16 [16384, 4096], P('dp'), may hold values from -6 to 6
- target: bfloat16 [16384, 4096], P('dp'), may hold values from -4 to 4
- query_weight: bfloat16 [4096, 4096], P('dp', 'mp'), may hold values from -0.125 to 0.125
- key_weight: bfloat16 [4096, 1024], P('dp', 'mp'), may hold values from -0.125 to 0.125
- value_weight: bfloat16 [4096, 1024], P('dp', 'mp'), may hold values from -0.125 to 0.125
- out_weight: bfloat16 [4096, 4096], P('mp', 'dp'), may hold values from -0.25 to 0.25
- query_codes: int32 [1024, 4096], P('dp', 'mp'), may hold values from 0 to 5
- key_codes: int32 [1024, 1024], P('dp', 'mp'), may hold values from 0 to 5
- value_codes: int32 [1024, 1024], P('dp', 'mp'), may hold values from 0 to 5
- out_codes: int32 [1024, 4096], P('mp', 'dp'), may hold values from 0 to 5
- doc_lengths: int32 [64, 3], P('dp'), may hold values from 1 to 192, 256 in all within a row
Outputs:
- block_out: bfloat16 [16384, 4096], P('dp', 'mp')
- grad_key: float32 [4096, 1024], P('dp', 'mp')
The draws below stay inside these ranges and needn't reach their ends.
Inputs may be any that keep to these rules, and one draw needn't show every extreme that they name: `query_codes`: codes name which two of four consecutive rows a column keeps, as in the reference program. `key_codes`: codes as for query_codes. `value_codes`: codes as for query_codes. `out_codes`: codes as for query_codes. `doc_lengths`: each row sums to 256; its last entry is the count of padding slots.
All inputs are finite; a program needn't handle non-finite values.
Results may differ from the reference program's by a relative error of at most 0.015.
Values may be sent and summed in bfloat16 or wider, within the bound.
No kernel may reach another device: no remote copies, remote signals or barrier semaphores. Data moves between devices by JAX's collectives and lax.ppermute only.
A program may use at most 64 MiB of HBM per device.

```python
import math
import jax
import jax.numpy as jnp
import numpy as np
from jax import lax

D = 4096
HEADS = 32
KV_HEADS = 8
HEAD_DIM = 128
TOK_DEV = 256
DOCS_DEV = 2
LOSS_DIV = 16
TOKENS = 16384
N_DP = 64
N_MP = 8


def set_ends(values, stream_key, smallest, largest):
    shape = values.shape
    spot = [jax.random.randint(jax.random.fold_in(stream_key, axis), (), 0, shape[axis]) for axis in range(len(shape))]
    values = values.at[tuple(spot)].set(smallest)
    longest = shape.index(max(shape))
    spot[longest] = (spot[longest] + 1) % shape[longest]
    return values.at[tuple(spot)].set(largest)


def block_levels(rng, shape, cuts, least, high):
    loudness = 1.0
    for axis_at, shards_of in cuts:
        steps = jax.random.uniform(jax.random.fold_in(jax.random.fold_in(rng, 6), axis_at), (shards_of,), jnp.float32, least / len(cuts), high / len(cuts))
        loudness = loudness * jnp.repeat(jnp.exp(steps), shape[axis_at] // shards_of).reshape((-1,) + (1,) * (len(shape) - 1 - axis_at))
    return loudness


def split_up(number_of, total, most, slope):
    loads = [(1 << 20) // math.isqrt(grade ** slope) + 1 for grade in range(2, number_of + 1)]
    rest, counts = total - most - (number_of - 1), [1] * (number_of - 1)
    while rest > 0:
        free = [i for i in range(number_of - 1) if counts[i] < most]
        whole, remaining = sum([loads[i] for i in free]), rest
        for i in free:
            addition = min(most - counts[i], max(1, remaining * loads[i] // whole), rest)
            counts[i] = counts[i] + addition
            rest = rest - addition
    return np.array([most] + counts)


def ragged_sizes(stream_key, number_of, total, reach, slope):
    if number_of == 2:
        one = jax.random.randint(stream_key, (), max(1, total - reach), min(reach, total - 1) + 1)
        return jnp.stack([one, total - one])
    sizes = jnp.asarray(split_up(number_of, total, reach, slope), jnp.int32)
    pairs = (number_of - 1) // 2
    giver, receiver = sizes[1:1 + 2 * pairs:2], sizes[2:2 + 2 * pairs:2]
    slack = jnp.minimum(giver - 1, reach - receiver)
    moved = jax.random.randint(jax.random.fold_in(stream_key, 1), (pairs,), 0, 1 << 20) % (slack + 1)
    sizes = sizes.at[1:1 + 2 * pairs:2].set(giver - moved).at[2:2 + 2 * pairs:2].set(receiver + moved)
    return sizes[jax.random.permutation(jax.random.fold_in(stream_key, 2), number_of)]


def centred(key, dims, scale, reach, shards=(), kind=jnp.bfloat16):
    level = block_levels(key, dims, shards, -0.22, 0.18) if shards else 1.0
    entries = jax.random.normal(key, dims, jnp.float32) * scale * level
    return jnp.minimum(jnp.maximum(entries, -reach), reach).astype(kind)


def setup_inputs(seed: int = 0) -> dict:
    keys = jax.random.split(jax.random.key(seed), 12)
    return {
        "hidden": centred(keys[0], (TOKENS, D), 1.0, 6.0, ((0, 64),)),
        "target": centred(keys[1], (TOKENS, D), 0.5, 4.0, ((0, 64),)),
        "query_weight": centred(keys[2], (D, HEADS * HEAD_DIM), (D // 2) ** -0.5, 0.125, ((0, 64), (1, 8))),
        "key_weight": centred(keys[3], (D, KV_HEADS * HEAD_DIM), (D // 2) ** -0.5, 0.125, ((0, 64), (1, 8))),
        "value_weight": centred(keys[4], (D, KV_HEADS * HEAD_DIM), (D // 2) ** -0.5, 0.125, ((0, 64), (1, 8))),
        "out_weight": centred(keys[5], (HEADS * HEAD_DIM, D), (HEADS * HEAD_DIM // 8) ** -0.5, 0.25, ((0, 8), (1, 64))),
        "query_codes": set_ends(jax.random.randint(keys[6], (D // 4, HEADS * HEAD_DIM), 0, 6), jax.random.fold_in(keys[6], 1), 0, 5).astype(jnp.int32),
        "key_codes": set_ends(jax.random.randint(keys[7], (D // 4, KV_HEADS * HEAD_DIM), 0, 6), jax.random.fold_in(keys[7], 1), 0, 5).astype(jnp.int32),
        "value_codes": set_ends(jax.random.randint(keys[8], (D // 4, KV_HEADS * HEAD_DIM), 0, 6), jax.random.fold_in(keys[8], 1), 0, 5).astype(jnp.int32),
        "out_codes": set_ends(jax.random.randint(keys[9], (HEADS * HEAD_DIM // 4, D), 0, 6), jax.random.fold_in(keys[9], 1), 0, 5).astype(jnp.int32),
        "doc_lengths": jax.vmap(lambda own: ragged_sizes(own, DOCS_DEV + 1, TOK_DEV, TOK_DEV * 3 // 4, 2))(jax.random.split(keys[10], N_DP)).reshape((N_DP, DOCS_DEV + 1)).astype(jnp.int32),
    }


KEPT_PAIRS = ((0, 1), (0, 2), (0, 3), (1, 2), (1, 3), (2, 3))
ROPE_BASE = 500000.0


def apply_mask(weight, group_codes):
    chosen_rows = []
    for within in range(4):
        chosen = jnp.zeros(group_codes.shape, jnp.bool_)
        for number, kept_pair in enumerate(KEPT_PAIRS):
            if within in kept_pair:
                chosen = chosen | (group_codes == number)
        chosen_rows.append(chosen)
    keep_mask = jnp.stack(chosen_rows, axis=1).reshape(weight.shape)
    return jnp.where(keep_mask, weight, jnp.zeros_like(weight))


def doc_layout(lengths, row_total):
    doc_ends = jnp.cumsum(lengths, dtype=jnp.int32)
    positions = jnp.arange(row_total, dtype=jnp.int32)
    passed = positions[:, None] >= doc_ends[None, :]
    segment = jnp.sum(passed.astype(jnp.int32), axis=1, dtype=jnp.int32)
    begins = jnp.sum(jnp.where(passed, lengths[None, :], 0), axis=1, dtype=jnp.int32)
    return segment, positions - begins, segment < lengths.shape[0] - 1


def angles(doc_pos, head_dim):
    exponent = jnp.arange(head_dim // 2, dtype=jnp.float32) * (2.0 / head_dim)
    inverse_freq = jnp.power(jnp.float32(ROPE_BASE), -exponent)
    phases = doc_pos.astype(jnp.float32)[..., None] * inverse_freq
    return jnp.cos(phases)[..., None, :], jnp.sin(phases)[..., None, :]


def rotate(values, angle_cos, angle_sin):
    half_dim = values.shape[-1] // 2
    front_half = values[..., :half_dim]
    back_half = values[..., half_dim:]
    return jnp.concatenate([front_half * angle_cos - back_half * angle_sin,
                            back_half * angle_cos + front_half * angle_sin], axis=-1)


def probabilities(queries, key_heads, segment):
    row_total = queries.shape[0]
    scores = jnp.einsum('qkgd,skd->kgqs', queries.astype(jnp.float32), key_heads.astype(jnp.float32))
    scores = scores * (queries.shape[-1] ** -0.5)
    positions = jnp.arange(row_total)
    allowed = (segment[:, None] == segment[None, :]) & (positions[None, :] <= positions[:, None])
    raised = jnp.where(allowed, jnp.exp(scores), jnp.zeros_like(scores))
    return raised / jnp.sum(raised, axis=-1, keepdims=True)


def rank_forward(operands):
    queries, key_heads, values, segment = operands
    probability = probabilities(queries, key_heads, segment)
    rounded = lax.optimization_barrier(probability.astype(jnp.bfloat16)).astype(jnp.float32)
    result = jnp.einsum('kgqs,skd->qkgd', rounded, values.astype(jnp.float32))
    return result.reshape(queries.shape[0], -1).astype(jnp.bfloat16)


def rank_backward(operands):
    queries, key_heads, values, segment, d_attended = operands
    probability = probabilities(queries, key_heads, segment)
    d_prob = jnp.einsum('qkgd,skd->kgqs', d_attended.astype(jnp.float32), values.astype(jnp.float32))
    row_dot = jnp.sum(probability * d_prob, axis=-1, keepdims=True)
    d_score = (probability * (d_prob - row_dot) * (queries.shape[-1] ** -0.5)).astype(jnp.bfloat16)
    d_score = lax.optimization_barrier(d_score).astype(jnp.float32)
    return jnp.einsum('kgqs,qkgd->skd', d_score, queries.astype(jnp.float32))


def reference(hidden, target, query_weight, key_weight, value_weight, out_weight,
              query_codes, key_codes, value_codes, out_codes, doc_lengths):
    masked_query = apply_mask(query_weight, query_codes)
    masked_key = apply_mask(key_weight, key_codes)
    masked_value = apply_mask(value_weight, value_codes)
    masked_out = apply_mask(out_weight, out_codes)
    query_raw = jnp.dot(hidden, masked_query, preferred_element_type=jnp.float32)
    key_raw = jnp.dot(hidden, masked_key, preferred_element_type=jnp.float32)
    value_raw = jnp.dot(hidden, masked_value, preferred_element_type=jnp.float32)
    segment, doc_pos, live_rows = jax.vmap(doc_layout, in_axes=(0, None))(doc_lengths, TOK_DEV)
    angle_cos, angle_sin = angles(doc_pos, HEAD_DIM)
    group_size = HEADS // KV_HEADS
    queries = rotate(query_raw.reshape(N_DP, TOK_DEV, HEADS, HEAD_DIM), angle_cos, angle_sin)
    queries = queries.astype(jnp.bfloat16).reshape(N_DP, TOK_DEV, KV_HEADS, group_size, HEAD_DIM)
    key_heads = rotate(key_raw.reshape(N_DP, TOK_DEV, KV_HEADS, HEAD_DIM), angle_cos, angle_sin).astype(jnp.bfloat16)
    values = value_raw.astype(jnp.bfloat16).reshape(N_DP, TOK_DEV, KV_HEADS, HEAD_DIM)
    attended = lax.map(rank_forward, (queries, key_heads, values, segment)).reshape(TOKENS, HEADS * HEAD_DIM)
    local_width = HEADS * HEAD_DIM // N_MP
    out_total = jnp.zeros((TOKENS, D), jnp.float32)
    for member in range(N_MP):
        lower = member * local_width
        rounded_term = jnp.dot(attended[:, lower:lower + local_width], masked_out[lower:lower + local_width, :],
                               preferred_element_type=jnp.float32).astype(jnp.bfloat16)
        out_total = out_total + lax.optimization_barrier(rounded_term).astype(jnp.float32)
    block_out = out_total.astype(jnp.bfloat16)
    live_flat = live_rows.reshape(TOKENS, 1).astype(jnp.float32)
    out_error = ((out_total - target.astype(jnp.float32)) * live_flat / LOSS_DIV).astype(jnp.bfloat16)
    d_attended = jnp.dot(out_error, masked_out.T, preferred_element_type=jnp.float32).astype(jnp.bfloat16)
    d_attended = d_attended.reshape(N_DP, TOK_DEV, KV_HEADS, group_size, HEAD_DIM)
    d_key_rot = lax.map(rank_backward, (queries, key_heads, values, segment, d_attended))
    d_key = rotate(d_key_rot, angle_cos, -angle_sin).astype(jnp.bfloat16).reshape(TOKENS, KV_HEADS * HEAD_DIM)
    grad_full = jnp.dot(hidden.T, d_key, preferred_element_type=jnp.float32)
    grad_key = apply_mask(grad_full, key_codes)
    return (block_out, grad_key)
```

```python
import functools

import jax
import jax.numpy as jnp
from jax import lax
from jax.experimental import pallas as pl
from jax.experimental.pallas import tpu as pltpu
from jax.sharding import Mesh, PartitionSpec as P

HEAD_DIM = 128
LOSS_DIV = 16
ROPE_BASE = 500000.0
KEEP_BITS = (0b000111, 0b011001, 0b101010, 0b110100)
VMEM = pltpu.CompilerParams(vmem_limit_bytes=58 * 1024 * 1024)
F32 = jnp.float32
BF16 = jnp.bfloat16
NT = (((1,), (1,)), ((), ()))
TN = (((0,), (0,)), ((), ()))


def keep_mask(codes, rows):
    groups = codes.shape[0]
    at_row = lax.broadcasted_iota(jnp.int32, (rows, groups), 0)
    at_group = lax.broadcasted_iota(jnp.int32, (rows, groups), 1)
    spread = jnp.where(at_row // 4 == at_group, 1.0, 0.0).astype(BF16)
    wide = jnp.dot(spread, codes.astype(F32).astype(BF16), preferred_element_type=F32)
    wide = wide.astype(jnp.int32)
    within = lax.broadcasted_iota(jnp.int32, wide.shape, 0) % 4
    bits = jnp.where(
        within == 0,
        KEEP_BITS[0],
        jnp.where(within == 1, KEEP_BITS[1], jnp.where(within == 2, KEEP_BITS[2], KEEP_BITS[3])),
    )
    return (lax.shift_right_logical(bits, wide) & 1) == 1


def masked(weight, codes):
    kept = jnp.where(keep_mask(codes, weight.shape[0]), weight.astype(F32), 0.0)
    return kept.astype(BF16)


def mask_qkv_kernel(qw, kw, vw, qc, kc, vc, out):
    weight = jnp.concatenate([qw[...], kw[...], vw[...]], axis=1)
    codes = jnp.concatenate([qc[...], kc[...], vc[...]], axis=1)
    kept = masked(weight, codes)
    for copy in range(out.shape[0]):
        out[copy] = kept


def mask_out_kernel(ow, oc, out):
    kept = masked(ow[...], oc[...])
    cols = kept.shape[1]
    eye = lax.broadcasted_iota(jnp.int32, (cols, cols), 0) == lax.broadcasted_iota(
        jnp.int32, (cols, cols), 1
    )
    eye = jnp.where(eye, 1.0, 0.0).astype(BF16)
    out[...] = lax.dot_general(eye, kept, NT, preferred_element_type=F32).astype(BF16)


def split_hidden_kernel(at_ref, hidden, out):
    shifts, tokens, width = out.shape
    n_z = width // 128
    half = width // 2
    low = lax.broadcasted_iota(jnp.int32, (tokens, 128), 1) < 64
    own = low == (at_ref[1] == 0)
    for shift in range(shifts):
        y_to = lax.rem(at_ref[0] + shift, shifts)
        for pair in range(n_z // 2):
            both = []
            for z in (2 * pair, 2 * pair + 1):
                lane = pl.multiple_of((z * shifts + y_to) * 128, 128)
                both.append(hidden[:, pl.ds(lane, 128)].astype(F32))
            mine = [jnp.where(own, v, pltpu.roll(v, 64, 1)) for v in both]
            rest = [jnp.where(own, pltpu.roll(v, 64, 1), v) for v in both]
            for part, (first, last) in enumerate((mine, rest)):
                start = part * half + pair * 128
                out[shift, :, start : start + 128] = jnp.where(low, first, last).astype(BF16)


def rotate(values, cos, sin):
    return values * cos + pltpu.roll(values, HEAD_DIM // 2, 1) * sin


def project_kernel(w_own, w_oth, s0, s1, s2, s3, p0, p1, p2, p3):
    half = w_own.shape[0]
    for slot, term in ((s2, p2), (s1, p1), (s3, p3), (s0, p0)):
        total = jnp.dot(slot[:, :half], w_own[...], preferred_element_type=F32)
        total += jnp.dot(slot[:, half:], w_oth[...], preferred_element_type=F32)
        term[...] = total.astype(term.dtype)


def attend_kernel(p0, p1, p2, p3, cos, sin, allow, q_out, v_out, prob_out, att_out):
    raw = p0[...] + p1[...].astype(F32) + p2[...].astype(F32) + p3[...].astype(F32)
    heads = q_out.shape[1] // HEAD_DIM
    at = heads * HEAD_DIM
    keys = rotate(raw[:, at : at + HEAD_DIM], cos[...], sin[...]).astype(BF16)
    values = raw[:, at + HEAD_DIM :].astype(BF16)
    v_out[...] = values
    for head in range(heads):
        cut = slice(head * HEAD_DIM, (head + 1) * HEAD_DIM)
        query = rotate(raw[:, cut], cos[...], sin[...]).astype(BF16)
        q_out[:, cut] = query
        scores = lax.dot_general(query, keys, NT, preferred_element_type=F32)
        raised = jnp.where(allow[...] > 0.5, jnp.exp(scores * HEAD_DIM**-0.5), 0.0)
        prob = raised / jnp.sum(raised, axis=1, keepdims=True)
        prob_out[head] = prob
        att_out[:, cut] = jnp.dot(prob.astype(BF16), values, preferred_element_type=F32).astype(
            BF16
        )


def key_grad_kernel(d_own, d_other, q_ref, v_ref, prob_ref, cos, sin, out):
    d_att = (d_own[...] + d_other[...].astype(F32)).astype(BF16)
    total = jnp.zeros(out.shape, F32)
    for head in range(prob_ref.shape[0]):
        cut = slice(head * HEAD_DIM, (head + 1) * HEAD_DIM)
        d_prob = lax.dot_general(d_att[:, cut], v_ref[...], NT, preferred_element_type=F32)
        prob = prob_ref[head]
        row_dot = jnp.sum(prob * d_prob, axis=1, keepdims=True)
        d_score = (prob * (d_prob - row_dot) * HEAD_DIM**-0.5).astype(BF16)
        total += lax.dot_general(d_score, q_ref[:, cut], TN, preferred_element_type=F32)
    out[...] = rotate(total, cos[...], -sin[...]).astype(BF16)


def out_block(pieces, k, r):
    return jnp.concatenate([piece[k, r] for piece in pieces], axis=0)


def out_kernel(at_ref, own, oth, *refs):
    pieces, out = refs[:-1], refs[-1]
    zh = at_ref[2]
    for k in range(out.shape[0]):
        total = lax.dot_general(own[...], out_block(pieces, k, zh), NT, preferred_element_type=F32)
        total += lax.dot_general(
            oth[...], out_block(pieces, k, 1 - zh), NT, preferred_element_type=F32
        )
        out[k] = total.astype(out.dtype)


def d_att_kernel(which, at_ref, errors, *refs):
    pieces, out = refs[:-1], refs[-1]
    r = at_ref[2] if which == 0 else 1 - at_ref[2]
    total = jnp.zeros(out.shape, F32)
    for k in range(errors.shape[0]):
        total += jnp.dot(errors[k], out_block(pieces, k, r), preferred_element_type=F32)
    out[...] = total.astype(out.dtype)


def error_kernel(at_ref, blocks, target, live, block_out, errors):
    tokens = target.shape[0]
    n_y = target.shape[1] // 128
    swap = at_ref[1] == 1
    for shift in range(n_y):
        y_from = lax.rem(at_ref[0] + n_y - shift, n_y)
        lane = pl.multiple_of(y_from * 128, 128)
        cut = slice(shift * 128, (shift + 1) * 128)
        total = jnp.sum(blocks[:, :, cut].astype(F32), axis=0)
        placed = jnp.where(swap, pltpu.roll(total, 64, 1), total)
        block_out[:, pl.ds(lane, 128)] = placed.astype(BF16)
        want = target[:, pl.ds(lane, 128)].astype(F32)
        want = jnp.where(swap, pltpu.roll(want, 64, 1), want)
        error = ((total - want) * live[...] / LOSS_DIV).astype(BF16)
        for k in range(errors.shape[0]):
            errors[k, :, cut] = error


def grad_kernel(s0, s1, s2, s3, d0, d1, d2, d3, own, oth):
    half = own.shape[0]
    for at, out in ((0, own), (half, oth)):
        total = jnp.zeros(out.shape, F32)
        for slot, d_key in ((s0, d0), (s1, d1), (s2, d2), (s3, d3)):
            total += lax.dot_general(
                slot[:, at : at + half], d_key[...], TN, preferred_element_type=F32
            )
        out[...] = total.astype(out.dtype)


def final_kernel(parts, codes, out):
    total = jnp.sum(parts[...].astype(F32), axis=0)
    out[...] = jnp.where(keep_mask(codes[...], out.shape[0]), total, 0.0)


def doc_layout(lengths, row_total):
    doc_ends = jnp.cumsum(lengths, dtype=jnp.int32)
    positions = jnp.arange(row_total, dtype=jnp.int32)
    passed = positions[:, None] >= doc_ends[None, :]
    segment = jnp.sum(passed.astype(jnp.int32), axis=1, dtype=jnp.int32)
    begins = jnp.sum(jnp.where(passed, lengths[None, :], 0), axis=1, dtype=jnp.int32)
    return segment, positions - begins, segment < lengths.shape[0] - 1


def angles(doc_pos):
    exponent = jnp.arange(HEAD_DIM // 2, dtype=F32) * (2.0 / HEAD_DIM)
    phases = doc_pos.astype(F32)[:, None] * jnp.power(F32(ROPE_BASE), -exponent)
    cos, sin = jnp.cos(phases), jnp.sin(phases)
    return jnp.concatenate([cos, cos], axis=1), jnp.concatenate([-sin, sin], axis=1)


def call(kernel, out_shape, *args, at=None):
    specs = [pl.BlockSpec(memory_space=pltpu.VMEM)] * len(args)
    if at is not None:
        args, specs = (at,) + args, [pl.BlockSpec(memory_space=pltpu.SMEM)] + specs
    return pl.pallas_call(kernel, out_shape=out_shape, in_specs=specs, compiler_params=VMEM)(*args)


def shape(dims, kind=BF16):
    return jax.ShapeDtypeStruct(dims, kind)


def shifted(value, axis, by):
    size = lax.axis_size(axis)
    return lax.ppermute(value, axis, [(i, (i + by) % size) for i in range(size)])


def copies(value, count):
    return jnp.broadcast_to(value[None], (count,) + value.shape)


def after(value, *earlier):
    return lax.optimization_barrier((value,) + earlier)[0]


def shards(hidden, target, qw, kw, vw, ow, qc, kc, vc, oc, doc_lengths):
    tokens = hidden.shape[0]
    n_z, n_y, n_c, n_x = (lax.axis_size(a) for a in ("zl", "y", "c", "x"))
    y_at, c_at, zh_at, x_at = (lax.axis_index(a) for a in ("y", "c", "zh", "x"))
    at = jnp.stack([y_at, c_at, zh_at])
    rows, q_width = qw.shape
    width = q_width + 2 * kw.shape[1]
    heads = q_width // HEAD_DIM
    depth = n_z * n_c * rows

    mine = call(mask_qkv_kernel, shape((n_z, rows, width)), qw, kw, vw, qc, kc, vc)
    w_own = lax.all_to_all(mine, "zl", 0, 0)

    split = call(split_hidden_kernel, shape((n_y, tokens, depth)), hidden, at=at)
    slots = [split[0]] + [shifted(split[s], "y", s) for s in range(1, n_y)]
    w_own, *slots = lax.optimization_barrier((w_own, *slots))

    out_mine = call(mask_out_kernel, shape((ow.shape[1], ow.shape[0])), ow, oc)
    trade = []
    for z in range(n_z):
        for half in range(2):
            other = (z - 1 if half == 0 else z + 1) * 2 + 1 - half
            trade.append((z * 2 + half, other if z % 2 != half else z * 2 + half))
    out_mine = lax.ppermute(out_mine, ("zl", "zh"), trade)
    out_mine = after(out_mine, w_own)
    out_z = lax.all_to_all(copies(out_mine, n_z), "zl", 0, 0)

    w_oth = shifted(w_own, "c", 1)
    terms = call(
        project_kernel,
        [shape((tokens, width), F32)] + [shape((tokens, width))] * (n_y - 1),
        w_own.reshape(-1, width),
        w_oth.reshape(-1, width),
        *slots,
    )
    terms = [terms[0]] + [shifted(terms[s], "y", -s) for s in range(1, n_y)]

    out_z = after(out_z, *terms).reshape(n_z // 2, 2, ow.shape[1], ow.shape[0])
    out_y = [out_z] + [shifted(out_z, "y", s) for s in range(1, n_y)]
    pieces = []
    for piece in out_y:
        pieces += [piece, shifted(piece, "c", 1)]

    segment, doc_pos, live = doc_layout(doc_lengths[0], tokens)
    cos, sin = angles(doc_pos)
    spot = jnp.arange(tokens)
    allow = (segment[:, None] == segment[None, :]) & (spot[None, :] <= spot[:, None])
    queries, values, prob, att = call(
        attend_kernel,
        (
            shape((tokens, q_width)),
            shape((tokens, HEAD_DIM)),
            shape((heads, tokens, tokens), F32),
            shape((tokens, q_width)),
        ),
        *terms,
        cos,
        sin,
        allow.astype(F32),
    )

    att_oth = shifted(att, "zh", 1)
    block = target.shape[1] // (n_x * 2)
    part = call(out_kernel, shape((n_x, tokens, block)), att, att_oth, *pieces, at=at)
    blocks = lax.all_to_all(part, "x", 0, 0)
    target_share = lax.dynamic_slice_in_dim(target, (x_at * 2 + zh_at) * block, block, 1)
    block_out, error = call(
        error_kernel,
        (shape((tokens, block)), shape((n_x, tokens, block))),
        blocks,
        target_share,
        live[:, None].astype(F32),
        at=at,
    )
    errors = lax.all_to_all(error, "x", 0, 0)
    d_oth = call(functools.partial(d_att_kernel, 1), shape(att.shape), errors, *pieces, at=at)
    d_oth = shifted(d_oth, "zh", 1)
    d_own = call(functools.partial(d_att_kernel, 0), shape(att.shape, F32), errors, *pieces, at=at)

    d_key = call(
        key_grad_kernel, shape((tokens, HEAD_DIM)), d_own, d_oth, queries, values, prob, cos, sin
    )
    d_keys = [d_key] + [shifted(d_key, "y", s) for s in range(1, n_y)]
    half = (depth // 2, HEAD_DIM)
    g_own, g_oth = call(grad_kernel, (shape(half, F32), shape(half)), *slots, *d_keys)
    grad = (g_own + shifted(g_oth, "c", 1).astype(F32)).astype(BF16)
    grad = lax.all_to_all(grad.reshape(n_z, rows, HEAD_DIM), "zl", 0, 0)
    grad_key = call(final_kernel, shape((rows, HEAD_DIM), F32), grad, kc)
    return block_out, grad_key


def solution(mesh):
    fine = Mesh(mesh.devices.reshape(8, 4, 2, 4, 2), ("zl", "y", "c", "x", "zh"))
    dp, mp = ("zl", "y", "c"), ("x", "zh")
    by_dp, by_both, by_mp = P(dp, None), P(dp, mp), P(mp, dp)
    placed = (by_dp, by_dp) + (by_both,) * 3 + (by_mp,) + (by_both,) * 3 + (by_mp, by_dp)
    return jax.shard_map(
        shards, mesh=fine, in_specs=placed, out_specs=(by_both, by_both), check_vma=False
    )
```

```python
import functools

import jax
import jax.numpy as jnp
from jax import lax
from jax.experimental import pallas as pl
from jax.experimental.pallas import tpu as pltpu
from jax.sharding import Mesh, PartitionSpec as P

HEAD_DIM = 128
LOSS_DIV = 16
ROPE_BASE = 500000.0
KEEP_BITS = (0b000111, 0b011001, 0b101010, 0b110100)
MIB = 1024 * 1024
F32 = jnp.float32
BF16 = jnp.bfloat16
NT = (((1,), (1,)), ((), ()))
TN = (((0,), (0,)), ((), ()))


def keep_mask(codes, rows):
    groups = codes.shape[0]
    at_row = lax.broadcasted_iota(jnp.int32, (rows, groups), 0)
    at_group = lax.broadcasted_iota(jnp.int32, (rows, groups), 1)
    spread = jnp.where(at_row // 4 == at_group, 1.0, 0.0).astype(BF16)
    wide = jnp.dot(spread, codes.astype(F32).astype(BF16), preferred_element_type=F32)
    wide = wide.astype(jnp.int32)
    within = lax.broadcasted_iota(jnp.int32, wide.shape, 0) % 4
    bits = jnp.where(
        within == 0,
        KEEP_BITS[0],
        jnp.where(within == 1, KEEP_BITS[1], jnp.where(within == 2, KEEP_BITS[2], KEEP_BITS[3])),
    )
    return (lax.shift_right_logical(bits, wide) & 1) == 1


def masked(weight, codes):
    kept = jnp.where(keep_mask(codes, weight.shape[0]), weight.astype(F32), 0.0)
    return kept.astype(BF16)


def mask_qkv_kernel(qw, kw, vw, qc, kc, vc, out):
    weight = jnp.concatenate([qw[...], kw[...], vw[...]], axis=1)
    codes = jnp.concatenate([qc[...], kc[...], vc[...]], axis=1)
    kept = masked(weight, codes)
    for copy in range(out.shape[0]):
        out[copy] = kept


def mask_out_kernel(ow, oc, out):
    kept = masked(ow[...], oc[...])
    cols = kept.shape[1]
    eye = lax.broadcasted_iota(jnp.int32, (cols, cols), 0) == lax.broadcasted_iota(
        jnp.int32, (cols, cols), 1
    )
    eye = jnp.where(eye, 1.0, 0.0).astype(BF16)
    out[...] = lax.dot_general(eye, kept, NT, preferred_element_type=F32).astype(BF16)


def split_hidden_kernel(at_ref, hidden, *outs):
    shifts = len(outs)
    tokens, width = outs[0].shape
    n_z = width // 128
    half = width // 2
    low = lax.broadcasted_iota(jnp.int32, (tokens, 128), 1) < 64
    own = low == (at_ref[2] == 0)
    for shift in range(shifts):
        y_to = lax.rem(at_ref[0] + shift, shifts)
        for pair in range(n_z // 2):
            both = []
            for z in (2 * pair, 2 * pair + 1):
                lane = pl.multiple_of((z * shifts + y_to) * 128, 128)
                both.append(hidden[:, pl.ds(lane, 128)].astype(F32))
            mine = [jnp.where(own, v, pltpu.roll(v, 64, 1)) for v in both]
            rest = [jnp.where(own, pltpu.roll(v, 64, 1), v) for v in both]
            for part, (first, last) in enumerate((mine, rest)):
                start = part * half + pair * 128
                outs[shift][:, start : start + 128] = jnp.where(low, first, last).astype(BF16)


def rotate(values, cos, sin):
    return values * cos + pltpu.roll(values, HEAD_DIM // 2, 1) * sin


def project_kernel(w_own, w_oth, s0, s1, s2, s3, p0, p1, p2, p3):
    half = w_own.shape[0]
    for slot, term in ((s2, p2), (s1, p1), (s3, p3), (s0, p0)):
        total = jnp.dot(slot[:, :half], w_own[...], preferred_element_type=F32)
        total += jnp.dot(slot[:, half:], w_oth[...], preferred_element_type=F32)
        term[...] = total.astype(term.dtype)


def attend_kernel(p0, p1, p2, p3, cos, sin, allow, q_out, v_out, prob_out, att_out):
    raw = p0[...] + p1[...].astype(F32) + p2[...].astype(F32) + p3[...].astype(F32)
    heads = q_out.shape[1] // HEAD_DIM
    at = heads * HEAD_DIM
    keys = rotate(raw[:, at : at + HEAD_DIM], cos[...], sin[...]).astype(BF16)
    values = raw[:, at + HEAD_DIM :].astype(BF16)
    v_out[...] = values
    for head in range(heads):
        cut = slice(head * HEAD_DIM, (head + 1) * HEAD_DIM)
        query = rotate(raw[:, cut], cos[...], sin[...]).astype(BF16)
        q_out[:, cut] = query
        scores = lax.dot_general(query, keys, NT, preferred_element_type=F32)
        raised = jnp.where(allow[...] > 0.5, jnp.exp(scores * HEAD_DIM**-0.5), 0.0)
        prob = raised / jnp.sum(raised, axis=1, keepdims=True)
        prob_out[head] = prob
        att_out[:, cut] = jnp.dot(prob.astype(BF16), values, preferred_element_type=F32).astype(
            BF16
        )


def key_grad_kernel(d_own, d_other, q_ref, v_ref, prob_ref, cos, sin, out):
    d_att = (d_own[...] + d_other[...].astype(F32)).astype(BF16)
    total = jnp.zeros(out.shape[1:], F32)
    for head in range(prob_ref.shape[0]):
        cut = slice(head * HEAD_DIM, (head + 1) * HEAD_DIM)
        d_prob = lax.dot_general(d_att[:, cut], v_ref[...], NT, preferred_element_type=F32)
        prob = prob_ref[head]
        row_dot = jnp.sum(prob * d_prob, axis=1, keepdims=True)
        d_score = (prob * (d_prob - row_dot) * HEAD_DIM**-0.5).astype(BF16)
        total += lax.dot_general(d_score, q_ref[:, cut], TN, preferred_element_type=F32)
    d_key = rotate(total, cos[...], -sin[...]).astype(BF16)
    for copy in range(out.shape[0]):
        out[copy] = d_key


def out_block(weight, k, r):
    return jnp.concatenate([weight[part, k, r] for part in range(weight.shape[0])], axis=0)


def out_kernel(at_ref, own, oth, weight, out):
    zh = at_ref[1]
    for k in range(out.shape[0]):
        total = lax.dot_general(own[...], out_block(weight, k, zh), NT, preferred_element_type=F32)
        total += lax.dot_general(oth[...], out_block(weight, k, 1 - zh), NT, preferred_element_type=F32)
        out[k] = total.astype(out.dtype)


def d_att_kernel(which, at_ref, errors, weight, out):
    r = at_ref[1] if which == 0 else 1 - at_ref[1]
    total = jnp.zeros(out.shape, F32)
    for k in range(errors.shape[0]):
        total += jnp.dot(errors[k], out_block(weight, k, r), preferred_element_type=F32)
    out[...] = total.astype(out.dtype)


def error_kernel(blocks, target, live, block_out, errors):
    total = jnp.sum(blocks[...].astype(F32), axis=0)
    block_out[...] = total.astype(BF16)
    error = ((total - target[...].astype(F32)) * live[...] / LOSS_DIV).astype(BF16)
    for k in range(errors.shape[0]):
        errors[k] = error


def grad_kernel(at_ref, s0, s1, s2, s3, d_keys, own, oth):
    half = own.shape[0]
    n_y = d_keys.shape[0]
    for at, out in ((half, oth), (0, own)):
        total = jnp.zeros(out.shape, F32)
        for shift, slot in enumerate((s0, s1, s2, s3)):
            d_key = d_keys[lax.rem(at_ref[0] + n_y - shift, n_y)]
            total += lax.dot_general(slot[:, at : at + half], d_key, TN, preferred_element_type=F32)
        out[...] = total.astype(out.dtype)


def final_kernel(parts, codes, out):
    total = jnp.sum(parts[...].astype(F32), axis=0)
    out[...] = jnp.where(keep_mask(codes[...], out.shape[0]), total, 0.0)


def doc_layout(lengths, row_total):
    doc_ends = jnp.cumsum(lengths, dtype=jnp.int32)
    positions = jnp.arange(row_total, dtype=jnp.int32)
    passed = positions[:, None] >= doc_ends[None, :]
    segment = jnp.sum(passed.astype(jnp.int32), axis=1, dtype=jnp.int32)
    begins = jnp.sum(jnp.where(passed, lengths[None, :], 0), axis=1, dtype=jnp.int32)
    return segment, positions - begins, segment < lengths.shape[0] - 1


def angles(doc_pos):
    exponent = jnp.arange(HEAD_DIM // 2, dtype=F32) * (2.0 / HEAD_DIM)
    phases = doc_pos.astype(F32)[:, None] * jnp.power(F32(ROPE_BASE), -exponent)
    cos, sin = jnp.cos(phases), jnp.sin(phases)
    return jnp.concatenate([cos, cos], axis=1), jnp.concatenate([-sin, sin], axis=1)


def call(kernel, out_shape, *args, at=None, mib=20, flops=None):
    specs = [pl.BlockSpec(memory_space=pltpu.VMEM)] * len(args)
    if at is not None:
        args, specs = (at,) + args, [pl.BlockSpec(memory_space=pltpu.SMEM)] + specs
    params = pltpu.CompilerParams(vmem_limit_bytes=mib * MIB)
    cost = flops and pl.CostEstimate(flops=flops, bytes_accessed=0, transcendentals=0)
    return pl.pallas_call(
        kernel, out_shape=out_shape, in_specs=specs, compiler_params=params, cost_estimate=cost
    )(*args)


def shape(dims, kind=BF16):
    return jax.ShapeDtypeStruct(dims, kind)


def shifted(value, axis, by):
    size = lax.axis_size(axis)
    return lax.ppermute(value, axis, [(i, (i + by) % size) for i in range(size)])


def copies(value, count):
    return jnp.broadcast_to(value[None], (count,) + value.shape)


def after(value, *earlier):
    return lax.optimization_barrier((value,) + earlier)[0]


def shards(hidden, target, qw, kw, vw, ow, qc, kc, vc, oc, doc_lengths):
    tokens = hidden.shape[0]
    n_z, n_y, n_c, n_x = (lax.axis_size(a) for a in ("zl", "y", "c", "x"))
    y_at, c_at, zh_at, x_at = (lax.axis_index(a) for a in ("y", "c", "zh", "x"))
    at = jnp.stack([y_at, zh_at, c_at])
    rows, q_width = qw.shape
    width = q_width + 2 * kw.shape[1]
    heads = q_width // HEAD_DIM
    depth = n_z * n_c * rows

    mine = call(mask_qkv_kernel, shape((n_z, rows, width)), qw, kw, vw, qc, kc, vc, mib=58)
    w_own = lax.all_to_all(mine, "zl", 0, 0)

    split = call(split_hidden_kernel, [shape((tokens, depth))] * n_y, hidden, at=at)
    slots = [split[0]] + [shifted(split[s], "y", s) for s in range(1, n_y)]
    w_own, *slots = lax.optimization_barrier((w_own, *slots))

    out_mine = call(mask_out_kernel, shape((ow.shape[1], ow.shape[0])), ow, oc)
    trade = []
    for z in range(n_z):
        for half in range(2):
            other = (z - 1 if half == 0 else z + 1) * 2 + 1 - half
            trade.append((z * 2 + half, other if z % 2 != half else z * 2 + half))
    out_mine = lax.ppermute(out_mine, ("zl", "zh"), trade)
    out_mine = after(out_mine, w_own)
    out_z = lax.all_to_all(copies(out_mine, n_z), "zl", 0, 0)

    w_oth = shifted(w_own, "c", 1)
    terms = call(
        project_kernel,
        [shape((tokens, width), F32)] + [shape((tokens, width))] * (n_y - 1),
        w_own.reshape(-1, width),
        w_oth.reshape(-1, width),
        *slots,
    )
    terms = [terms[0]] + [shifted(terms[s], "y", -s) for s in range(1, n_y)]

    out_z = after(out_z, *terms).reshape(n_z // 2, 2, ow.shape[1], ow.shape[0])
    out_w = lax.all_gather(out_z, ("y", "c"), axis=0)

    segment, doc_pos, live = doc_layout(doc_lengths[0], tokens)
    cos, sin = angles(doc_pos)
    spot = jnp.arange(tokens)
    allow = (segment[:, None] == segment[None, :]) & (spot[None, :] <= spot[:, None])
    queries, values, prob, att = call(
        attend_kernel,
        (
            shape((tokens, q_width)),
            shape((tokens, HEAD_DIM)),
            shape((heads, tokens, tokens), F32),
            shape((tokens, q_width)),
        ),
        *terms,
        cos,
        sin,
        allow.astype(F32),
        mib=58,
    )

    att_oth = shifted(att, "zh", 1)
    block = target.shape[1] // (n_x * 2)
    part = call(out_kernel, shape((n_x, tokens, block)), att, att_oth, out_w, at=at)
    blocks = lax.all_to_all(part, "x", 0, 0)
    target_share = lax.dynamic_slice_in_dim(target, (x_at * 2 + zh_at) * block, block, 1)
    block_out, error = call(
        error_kernel,
        (shape((tokens, block)), shape((n_x, tokens, block))),
        blocks,
        target_share,
        live[:, None].astype(F32),
    )
    errors = lax.all_to_all(error, "x", 0, 0)
    d_oth = call(functools.partial(d_att_kernel, 1), shape(att.shape), errors, out_w, at=at)
    d_oth = shifted(d_oth, "zh", 1)
    d_own = call(functools.partial(d_att_kernel, 0), shape(att.shape, F32), errors, out_w, at=at)

    d_key = call(
        key_grad_kernel, shape((n_y, tokens, HEAD_DIM)), d_own, d_oth, queries, values, prob, cos, sin
    )
    d_keys = lax.all_to_all(d_key, "y", 0, 0)
    half = (depth // 2, HEAD_DIM)
    g_own, g_oth = call(grad_kernel, (shape(half, F32), shape(half)), *slots, d_keys, at=at)
    grad = (g_own + shifted(g_oth, "c", 1).astype(F32)).astype(BF16)
    grad = lax.all_to_all(grad.reshape(n_z, rows, HEAD_DIM), "zl", 0, 0)
    grad_key = call(final_kernel, shape((rows, HEAD_DIM), F32), grad, kc)
    return block_out, grad_key


def solution(mesh):
    fine = Mesh(mesh.devices.reshape(8, 4, 2, 4, 2), ("zl", "y", "c", "x", "zh"))
    dp, mp = ("zl", "y", "c"), ("x", "zh")
    by_dp, by_both, by_mp = P(dp, None), P(dp, mp), P(mp, dp)
    placed = (by_dp, by_dp) + (by_both,) * 3 + (by_mp,) + (by_both,) * 3 + (by_mp, by_dp)
    return jax.shard_map(
        shards, mesh=fine, in_specs=placed, out_specs=(by_both, by_both), check_vma=False
    )
```

```python
import functools

import jax
import jax.numpy as jnp
from jax import lax
from jax.experimental import pallas as pl
from jax.experimental.pallas import tpu as pltpu
from jax.sharding import Mesh, PartitionSpec as P

HEAD_DIM = 128
LOSS_DIV = 16
ROPE_BASE = 500000.0
KEEP_BITS = (0b000111, 0b011001, 0b101010, 0b110100)
MIB = 1024 * 1024
F32 = jnp.float32
BF16 = jnp.bfloat16
NT = (((1,), (1,)), ((), ()))
TN = (((0,), (0,)), ((), ()))


def keep_mask(codes, rows):
    groups = codes.shape[0]
    at_row = lax.broadcasted_iota(jnp.int32, (rows, groups), 0)
    at_group = lax.broadcasted_iota(jnp.int32, (rows, groups), 1)
    spread = jnp.where(at_row // 4 == at_group, 1.0, 0.0).astype(BF16)
    wide = jnp.dot(spread, codes.astype(F32).astype(BF16), preferred_element_type=F32)
    wide = wide.astype(jnp.int32)
    within = lax.broadcasted_iota(jnp.int32, wide.shape, 0) % 4
    bits = jnp.where(
        within == 0,
        KEEP_BITS[0],
        jnp.where(within == 1, KEEP_BITS[1], jnp.where(within == 2, KEEP_BITS[2], KEEP_BITS[3])),
    )
    return (lax.shift_right_logical(bits, wide) & 1) == 1


def masked(weight, codes):
    kept = jnp.where(keep_mask(codes, weight.shape[0]), weight.astype(F32), 0.0)
    return kept.astype(BF16)


def compact_qkv_kernel(qw, kw, vw, qc, kc, vc, out):
    weight = jnp.concatenate([qw[...], kw[...], vw[...]], axis=1)
    codes = jnp.concatenate([qc[...], kc[...], vc[...]], axis=1)
    groups, rows = codes.shape[0], weight.shape[0]
    at_group = lax.broadcasted_iota(jnp.int32, (groups, rows), 0)
    at_row = lax.broadcasted_iota(jnp.int32, (groups, rows), 1)
    plane = []
    for within in range(4):
        pick = jnp.where(at_row == 4 * at_group + within, 1.0, 0.0).astype(BF16)
        plane.append(jnp.dot(pick, weight, preferred_element_type=F32))
    first = jnp.where(codes < 3, plane[0], jnp.where(codes < 5, plane[1], plane[2]))
    second = jnp.where((codes == 1) | (codes == 3), plane[2], plane[3])
    second = jnp.where(codes == 0, plane[1], second)
    kept = jnp.concatenate([first, second, codes.astype(F32)], axis=0).astype(BF16)
    for copy in range(out.shape[0]):
        out[copy] = kept


def spread(kept):
    pieces, rows, width = kept.shape
    groups = rows // 3
    first, second, code = (
        kept[:, at * groups : (at + 1) * groups, :].astype(F32).reshape(pieces * groups, width)
        for at in range(3)
    )
    mid = (code == 3) | (code == 4)
    planes = (
        jnp.where(code < 3, first, 0.0),
        jnp.where(code == 0, second, jnp.where(mid, first, 0.0)),
        jnp.where((code == 1) | (code == 3), second, jnp.where(code == 5, first, 0.0)),
        jnp.where((code == 2) | (code > 3), second, 0.0),
    )
    return jnp.concatenate(planes, axis=0).astype(BF16)


def mask_out_kernel(ow, oc, out):
    kept = masked(ow[...], oc[...])
    cols = kept.shape[1]
    eye = lax.broadcasted_iota(jnp.int32, (cols, cols), 0) == lax.broadcasted_iota(
        jnp.int32, (cols, cols), 1
    )
    eye = jnp.where(eye, 1.0, 0.0).astype(BF16)
    out[...] = lax.dot_general(eye, kept, NT, preferred_element_type=F32).astype(BF16)


def split_hidden_kernel(at_ref, hidden, *outs):
    shifts = len(outs)
    depth = outs[0].shape[1]
    n_z = depth // 128
    row = lax.broadcasted_iota(jnp.int32, (depth, 1), 0)
    z, core, group, within = row // 128, row % 128 // 64, row % 64 // 4, row % 4
    place = jnp.where(core == at_ref[2], 0, depth // 2) + within * (depth // 8) + z * 16 + group
    column = lax.broadcasted_iota(jnp.int32, (depth, depth), 1)
    order = jnp.where(column == place, 1.0, 0.0).astype(BF16)
    for shift, out in enumerate(outs):
        y_to = lax.rem(at_ref[0] + shift, shifts)
        parts = []
        for z in range(n_z):
            lane = pl.multiple_of((z * shifts + y_to) * 128, 128)
            parts.append(hidden[:, pl.ds(lane, 128)])
        columns = jnp.concatenate(parts, axis=1)
        out[...] = jnp.dot(columns, order, preferred_element_type=F32).astype(BF16)


def rotate(values, cos, sin):
    return values * cos + pltpu.roll(values, HEAD_DIM // 2, 1) * sin


def project_kernel(w_own, w_oth, s0, s1, s2, s3, p0, p1, p2, p3):
    own, oth = spread(w_own), spread(w_oth)
    half = own.shape[0]
    for slot, term in ((s2, p2), (s1, p1), (s3, p3), (s0, p0)):
        total = jnp.dot(slot[:, :half], own, preferred_element_type=F32)
        total += jnp.dot(slot[:, half:], oth, preferred_element_type=F32)
        term[...] = total.astype(term.dtype)


def attend_kernel(p0, p1, p2, p3, cos, sin, allow, q_out, v_out, prob_out, att_out):
    raw = p0[...] + p1[...].astype(F32) + p2[...].astype(F32) + p3[...].astype(F32)
    heads = q_out.shape[1] // HEAD_DIM
    at = heads * HEAD_DIM
    keys = rotate(raw[:, at : at + HEAD_DIM], cos[...], sin[...]).astype(BF16)
    values = raw[:, at + HEAD_DIM :].astype(BF16)
    v_out[...] = values
    for head in range(heads):
        cut = slice(head * HEAD_DIM, (head + 1) * HEAD_DIM)
        query = rotate(raw[:, cut], cos[...], sin[...]).astype(BF16)
        q_out[:, cut] = query
        scores = lax.dot_general(query, keys, NT, preferred_element_type=F32)
        raised = jnp.where(allow[...] > 0.5, jnp.exp(scores * HEAD_DIM**-0.5), 0.0)
        prob = raised / jnp.sum(raised, axis=1, keepdims=True)
        prob_out[head] = prob
        att_out[:, cut] = jnp.dot(prob.astype(BF16), values, preferred_element_type=F32).astype(
            BF16
        )


def key_grad_kernel(d_own, d_other, q_ref, v_ref, prob_ref, cos, sin, out):
    d_att = (d_own[...] + d_other[...].astype(F32)).astype(BF16)
    total = jnp.zeros(out.shape[1:], F32)
    for head in range(prob_ref.shape[0]):
        cut = slice(head * HEAD_DIM, (head + 1) * HEAD_DIM)
        d_prob = lax.dot_general(d_att[:, cut], v_ref[...], NT, preferred_element_type=F32)
        prob = prob_ref[head]
        row_dot = jnp.sum(prob * d_prob, axis=1, keepdims=True)
        d_score = (prob * (d_prob - row_dot) * HEAD_DIM**-0.5).astype(BF16)
        total += lax.dot_general(d_score, q_ref[:, cut], TN, preferred_element_type=F32)
    d_key = rotate(total, cos[...], -sin[...]).astype(BF16)
    for copy in range(out.shape[0]):
        out[copy] = d_key


def out_block(weight, k, r):
    return jnp.concatenate([weight[part, k, r] for part in range(weight.shape[0])], axis=0)


def out_kernel(at_ref, own, oth, weight, out):
    zh = at_ref[1]
    for k in range(out.shape[0]):
        total = lax.dot_general(own[...], out_block(weight, k, zh), NT, preferred_element_type=F32)
        total += lax.dot_general(oth[...], out_block(weight, k, 1 - zh), NT, preferred_element_type=F32)
        out[k] = total.astype(out.dtype)


def d_att_kernel(which, at_ref, errors, weight, out):
    r = at_ref[1] if which == 0 else 1 - at_ref[1]
    total = jnp.zeros(out.shape, F32)
    for k in range(errors.shape[0]):
        total += jnp.dot(errors[k], out_block(weight, k, r), preferred_element_type=F32)
    out[...] = total.astype(out.dtype)


def error_kernel(blocks, target, live, block_out, errors):
    total = jnp.sum(blocks[...].astype(F32), axis=0)
    block_out[...] = total.astype(BF16)
    error = ((total - target[...].astype(F32)) * live[...] / LOSS_DIV).astype(BF16)
    for k in range(errors.shape[0]):
        errors[k] = error


def grad_kernel(at_ref, s0, s1, s2, s3, d_keys, own, oth):
    pieces, rows = own.shape[:2]
    half, groups = pieces * rows, rows // 4
    n_y = d_keys.shape[0]
    for at, out in ((half, oth), (0, own)):
        total = jnp.zeros((half, out.shape[2]), F32)
        for shift, slot in enumerate((s0, s1, s2, s3)):
            d_key = d_keys[lax.rem(at_ref[0] + n_y - shift, n_y)]
            total += lax.dot_general(slot[:, at : at + half], d_key, TN, preferred_element_type=F32)
        total = total.astype(out.dtype)
        for within in range(4):
            for z in range(pieces):
                start = (within * pieces + z) * groups
                out[z, within * groups : (within + 1) * groups] = total[start : start + groups]


def final_kernel(parts, codes, out):
    total = jnp.sum(parts[...].astype(F32), axis=0)
    groups = codes.shape[0]
    for within in range(4):
        keep = (lax.shift_right_logical(jnp.full(codes.shape, KEEP_BITS[within], jnp.int32), codes[...]) & 1) == 1
        rows = total[within * groups : (within + 1) * groups]
        out[pl.ds(within, groups, stride=4), :] = jnp.where(keep, rows, 0.0)


def doc_layout(lengths, row_total):
    doc_ends = jnp.cumsum(lengths, dtype=jnp.int32)
    positions = jnp.arange(row_total, dtype=jnp.int32)
    passed = positions[:, None] >= doc_ends[None, :]
    segment = jnp.sum(passed.astype(jnp.int32), axis=1, dtype=jnp.int32)
    begins = jnp.sum(jnp.where(passed, lengths[None, :], 0), axis=1, dtype=jnp.int32)
    return segment, positions - begins, segment < lengths.shape[0] - 1


def angles(doc_pos):
    exponent = jnp.arange(HEAD_DIM // 2, dtype=F32) * (2.0 / HEAD_DIM)
    phases = doc_pos.astype(F32)[:, None] * jnp.power(F32(ROPE_BASE), -exponent)
    cos, sin = jnp.cos(phases), jnp.sin(phases)
    return jnp.concatenate([cos, cos], axis=1), jnp.concatenate([-sin, sin], axis=1)


def call(kernel, out_shape, *args, at=None, mib=20, flops=None):
    specs = [pl.BlockSpec(memory_space=pltpu.VMEM)] * len(args)
    if at is not None:
        args, specs = (at,) + args, [pl.BlockSpec(memory_space=pltpu.SMEM)] + specs
    params = pltpu.CompilerParams(vmem_limit_bytes=mib * MIB)
    cost = flops and pl.CostEstimate(flops=flops, bytes_accessed=0, transcendentals=0)
    return pl.pallas_call(
        kernel, out_shape=out_shape, in_specs=specs, compiler_params=params, cost_estimate=cost
    )(*args)


def shape(dims, kind=BF16):
    return jax.ShapeDtypeStruct(dims, kind)


def shifted(value, axis, by):
    size = lax.axis_size(axis)
    return lax.ppermute(value, axis, [(i, (i + by) % size) for i in range(size)])


def copies(value, count):
    return jnp.broadcast_to(value[None], (count,) + value.shape)


def after(value, *earlier):
    return lax.optimization_barrier((value,) + earlier)[0]


def shards(hidden, target, qw, kw, vw, ow, qc, kc, vc, oc, doc_lengths):
    tokens = hidden.shape[0]
    n_z, n_y, n_c, n_x = (lax.axis_size(a) for a in ("zl", "y", "c", "x"))
    y_at, c_at, zh_at, x_at = (lax.axis_index(a) for a in ("y", "c", "zh", "x"))
    at = jnp.stack([y_at, zh_at, c_at])
    rows, q_width = qw.shape
    width = q_width + 2 * kw.shape[1]
    heads = q_width // HEAD_DIM
    depth = n_z * n_c * rows

    mine = call(compact_qkv_kernel, shape((n_z, 3 * rows // 4, width)), qw, kw, vw, qc, kc, vc, mib=58)
    w_own = lax.all_to_all(mine, "zl", 0, 0)

    split = call(split_hidden_kernel, [shape((tokens, depth))] * n_y, hidden, at=at, mib=40)
    slots = [split[0]] + [shifted(split[s], "y", s) for s in range(1, n_y)]
    segment, doc_pos, live = doc_layout(doc_lengths[0], tokens)
    cos, sin = angles(doc_pos)
    spot = jnp.arange(tokens)
    allow = (segment[:, None] == segment[None, :]) & (spot[None, :] <= spot[:, None])
    allow = allow.astype(F32)
    w_own, cos, sin, allow, *slots = lax.optimization_barrier((w_own, cos, sin, allow, *slots))

    out_mine = call(mask_out_kernel, shape((ow.shape[1], ow.shape[0])), ow, oc)
    trade = []
    for z in range(n_z):
        for half in range(2):
            other = (z - 1 if half == 0 else z + 1) * 2 + 1 - half
            trade.append((z * 2 + half, other if z % 2 != half else z * 2 + half))
    out_mine = lax.ppermute(out_mine, ("zl", "zh"), trade)
    out_mine = after(out_mine, w_own)
    out_z = lax.all_to_all(copies(out_mine, n_z), "zl", 0, 0)

    w_oth = shifted(w_own, "c", 1)
    terms = call(
        project_kernel,
        [shape((tokens, width), F32)] + [shape((tokens, width))] * (n_y - 1),
        w_own,
        w_oth,
        *slots,
    )
    terms = [terms[0]] + [shifted(terms[s], "y", -s) for s in range(1, n_y)]

    out_z = after(out_z, *terms).reshape(n_z // 2, 2, ow.shape[1], ow.shape[0])
    out_w = lax.all_gather(out_z, ("y", "c"), axis=0)

    queries, values, prob, att = call(
        attend_kernel,
        (
            shape((tokens, q_width)),
            shape((tokens, HEAD_DIM)),
            shape((heads, tokens, tokens), F32),
            shape((tokens, q_width)),
        ),
        *terms,
        cos,
        sin,
        allow,
        mib=58,
    )

    att_oth = shifted(att, "zh", 1)
    block = target.shape[1] // (n_x * 2)
    part = call(out_kernel, shape((n_x, tokens, block)), att, att_oth, out_w, at=at)
    blocks = lax.all_to_all(part, "x", 0, 0)
    target_share = lax.dynamic_slice_in_dim(target, (x_at * 2 + zh_at) * block, block, 1)
    block_out, error = call(
        error_kernel,
        (shape((tokens, block)), shape((n_x, tokens, block))),
        blocks,
        target_share,
        live[:, None].astype(F32),
    )
    errors = lax.all_to_all(error, "x", 0, 0)
    d_oth = call(functools.partial(d_att_kernel, 1), shape(att.shape), errors, out_w, at=at)
    d_oth = shifted(d_oth, "zh", 1)
    d_own = call(functools.partial(d_att_kernel, 0), shape(att.shape, F32), errors, out_w, at=at)

    d_key = call(
        key_grad_kernel, shape((n_y, tokens, HEAD_DIM)), d_own, d_oth, queries, values, prob, cos, sin
    )
    d_keys = lax.all_to_all(d_key, "y", 0, 0)
    half = (n_z, rows, HEAD_DIM)
    g_own, g_oth = call(grad_kernel, (shape(half, F32), shape(half)), *slots, d_keys, at=at)
    grad = (g_own + shifted(g_oth, "c", 1).astype(F32)).astype(BF16)
    grad = lax.all_to_all(grad, "zl", 0, 0)
    grad_key = call(final_kernel, shape((rows, HEAD_DIM), F32), grad, kc)
    return block_out, grad_key


def solution(mesh):
    fine = Mesh(mesh.devices.reshape(8, 4, 2, 4, 2), ("zl", "y", "c", "x", "zh"))
    dp, mp = ("zl", "y", "c"), ("x", "zh")
    by_dp, by_both, by_mp = P(dp, None), P(dp, mp), P(mp, dp)
    placed = (by_dp, by_dp) + (by_both,) * 3 + (by_mp,) + (by_both,) * 3 + (by_mp, by_dp)
    return jax.shard_map(
        shards, mesh=fine, in_specs=placed, out_specs=(by_both, by_both), check_vma=False
    )
```

```python
import functools

import jax
import jax.numpy as jnp
from jax import lax
from jax.experimental import pallas as pl
from jax.experimental.pallas import tpu as pltpu
from jax.sharding import Mesh, PartitionSpec as P

HEAD_DIM = 128
LOSS_DIV = 16
ROPE_BASE = 500000.0
KEEP_BITS = (0b000111, 0b011001, 0b101010, 0b110100)
MIB = 1024 * 1024
F32 = jnp.float32
BF16 = jnp.bfloat16
NT = (((1,), (1,)), ((), ()))
TN = (((0,), (0,)), ((), ()))


def keep_mask(codes, rows):
    groups = codes.shape[0]
    at_row = lax.broadcasted_iota(jnp.int32, (rows, groups), 0)
    at_group = lax.broadcasted_iota(jnp.int32, (rows, groups), 1)
    spread = jnp.where(at_row // 4 == at_group, 1.0, 0.0).astype(BF16)
    wide = jnp.dot(spread, codes.astype(F32).astype(BF16), preferred_element_type=F32)
    wide = wide.astype(jnp.int32)
    within = lax.broadcasted_iota(jnp.int32, wide.shape, 0) % 4
    bits = jnp.where(
        within == 0,
        KEEP_BITS[0],
        jnp.where(within == 1, KEEP_BITS[1], jnp.where(within == 2, KEEP_BITS[2], KEEP_BITS[3])),
    )
    return (lax.shift_right_logical(bits, wide) & 1) == 1


def masked(weight, codes):
    kept = jnp.where(keep_mask(codes, weight.shape[0]), weight.astype(F32), 0.0)
    return kept.astype(BF16)


def compact_qkv_kernel(qw, kw, vw, qc, kc, vc, out):
    weight = jnp.concatenate([qw[...], kw[...], vw[...]], axis=1)
    codes = jnp.concatenate([qc[...], kc[...], vc[...]], axis=1)
    groups, rows = codes.shape[0], weight.shape[0]
    at_group = lax.broadcasted_iota(jnp.int32, (groups, rows), 0)
    at_row = lax.broadcasted_iota(jnp.int32, (groups, rows), 1)
    plane = []
    for within in range(4):
        pick = jnp.where(at_row == 4 * at_group + within, 1.0, 0.0).astype(BF16)
        plane.append(jnp.dot(pick, weight, preferred_element_type=F32))
    first = jnp.where(codes < 3, plane[0], jnp.where(codes < 5, plane[1], plane[2]))
    second = jnp.where((codes == 1) | (codes == 3), plane[2], plane[3])
    second = jnp.where(codes == 0, plane[1], second)
    kept = jnp.concatenate([first, second, codes.astype(F32)], axis=0).astype(BF16)
    for copy in range(out.shape[0]):
        out[copy] = kept


def spread(kept):
    pieces, rows, width = kept.shape
    groups = rows // 3
    first, second, code = (
        kept[:, at * groups : (at + 1) * groups, :].astype(F32).reshape(pieces * groups, width)
        for at in range(3)
    )
    mid = (code == 3) | (code == 4)
    planes = (
        jnp.where(code < 3, first, 0.0),
        jnp.where(code == 0, second, jnp.where(mid, first, 0.0)),
        jnp.where((code == 1) | (code == 3), second, jnp.where(code == 5, first, 0.0)),
        jnp.where((code == 2) | (code > 3), second, 0.0),
    )
    return jnp.concatenate(planes, axis=0).astype(BF16)


def mask_out_kernel(ow, oc, out):
    kept = masked(ow[...], oc[...])
    cols = kept.shape[1]
    eye = lax.broadcasted_iota(jnp.int32, (cols, cols), 0) == lax.broadcasted_iota(
        jnp.int32, (cols, cols), 1
    )
    eye = jnp.where(eye, 1.0, 0.0).astype(BF16)
    out[...] = lax.dot_general(eye, kept, NT, preferred_element_type=F32).astype(BF16)


def split_hidden_kernel(at_ref, hidden, *outs):
    shifts = len(outs)
    depth = outs[0].shape[1]
    n_z = depth // 128
    row = lax.broadcasted_iota(jnp.int32, (depth, 1), 0)
    z, core, group, within = row // 128, row % 128 // 64, row % 64 // 4, row % 4
    place = jnp.where(core == at_ref[2], 0, depth // 2) + within * (depth // 8) + z * 16 + group
    column = lax.broadcasted_iota(jnp.int32, (depth, depth), 1)
    order = jnp.where(column == place, 1.0, 0.0).astype(BF16)
    for shift, out in enumerate(outs):
        y_to = lax.rem(at_ref[0] + shift, shifts)
        parts = []
        for z in range(n_z):
            lane = pl.multiple_of((z * shifts + y_to) * 128, 128)
            parts.append(hidden[:, pl.ds(lane, 128)])
        columns = jnp.concatenate(parts, axis=1)
        out[...] = jnp.dot(columns, order, preferred_element_type=F32).astype(BF16)


def rotate(values, cos, sin):
    return values * cos + pltpu.roll(values, HEAD_DIM // 2, 1) * sin


def project_kernel(w_own, w_oth, s0, s1, s2, s3, p0, p1, p2, p3):
    own, oth = spread(w_own), spread(w_oth)
    half = own.shape[0]
    for slot, term in ((s2, p2), (s1, p1), (s3, p3), (s0, p0)):
        total = jnp.dot(slot[:, :half], own, preferred_element_type=F32)
        total += jnp.dot(slot[:, half:], oth, preferred_element_type=F32)
        term[...] = total.astype(term.dtype)


def attend_kernel(p0, p1, p2, p3, cos, sin, allow, q_out, v_out, prob_out, att_out):
    raw = p0[...] + p1[...].astype(F32) + p2[...].astype(F32) + p3[...].astype(F32)
    heads = q_out.shape[1] // HEAD_DIM
    at = heads * HEAD_DIM
    keys = rotate(raw[:, at : at + HEAD_DIM], cos[...], sin[...]).astype(BF16)
    values = raw[:, at + HEAD_DIM :].astype(BF16)
    v_out[...] = values
    for head in range(heads):
        cut = slice(head * HEAD_DIM, (head + 1) * HEAD_DIM)
        query = rotate(raw[:, cut], cos[...], sin[...]).astype(BF16)
        q_out[:, cut] = query
        scores = lax.dot_general(query, keys, NT, preferred_element_type=F32)
        raised = jnp.where(allow[...] > 0.5, jnp.exp(scores * HEAD_DIM**-0.5), 0.0)
        prob = raised / jnp.sum(raised, axis=1, keepdims=True)
        prob_out[head] = prob
        att_out[:, cut] = jnp.dot(prob.astype(BF16), values, preferred_element_type=F32).astype(
            BF16
        )


def key_grad_kernel(d_own, d_other, q_ref, v_ref, prob_ref, cos, sin, out):
    d_att = (d_own[...] + d_other[...].astype(F32)).astype(BF16)
    total = jnp.zeros(out.shape[1:], F32)
    for head in range(prob_ref.shape[0]):
        cut = slice(head * HEAD_DIM, (head + 1) * HEAD_DIM)
        d_prob = lax.dot_general(d_att[:, cut], v_ref[...], NT, preferred_element_type=F32)
        prob = prob_ref[head]
        row_dot = jnp.sum(prob * d_prob, axis=1, keepdims=True)
        d_score = (prob * (d_prob - row_dot) * HEAD_DIM**-0.5).astype(BF16)
        total += lax.dot_general(d_score, q_ref[:, cut], TN, preferred_element_type=F32)
    d_key = rotate(total, cos[...], -sin[...]).astype(BF16)
    for copy in range(out.shape[0]):
        out[copy] = d_key


def out_block(weight, k, r):
    return jnp.concatenate([weight[part, k, r] for part in range(weight.shape[0])], axis=0)


def out_kernel(at_ref, own, oth, weight, out):
    zh = at_ref[1]
    for k in range(out.shape[0]):
        total = lax.dot_general(own[...], out_block(weight, k, zh), NT, preferred_element_type=F32)
        total += lax.dot_general(oth[...], out_block(weight, k, 1 - zh), NT, preferred_element_type=F32)
        out[k] = total.astype(out.dtype)


def d_att_kernel(which, at_ref, errors, weight, out):
    r = at_ref[1] if which == 0 else 1 - at_ref[1]
    total = jnp.zeros(out.shape, F32)
    for k in range(errors.shape[0]):
        total += jnp.dot(errors[k], out_block(weight, k, r), preferred_element_type=F32)
    out[...] = total.astype(out.dtype)


def error_kernel(blocks, target, live, block_out, errors):
    total = jnp.sum(blocks[...].astype(F32), axis=0)
    block_out[...] = total.astype(BF16)
    error = ((total - target[...].astype(F32)) * live[...] / LOSS_DIV).astype(BF16)
    for k in range(errors.shape[0]):
        errors[k] = error


def grad_kernel(at_ref, s0, s1, s2, s3, d_keys, own, oth):
    pieces, rows = own.shape[:2]
    half, groups = pieces * rows, rows // 4
    n_y = d_keys.shape[0]
    for at, out in ((half, oth), (0, own)):
        total = jnp.zeros((half, out.shape[2]), F32)
        for shift, slot in enumerate((s0, s1, s2, s3)):
            d_key = d_keys[lax.rem(at_ref[0] + n_y - shift, n_y)]
            total += lax.dot_general(slot[:, at : at + half], d_key, TN, preferred_element_type=F32)
        total = total.astype(out.dtype)
        for within in range(4):
            for z in range(pieces):
                start = (within * pieces + z) * groups
                out[z, within * groups : (within + 1) * groups] = total[start : start + groups]


def final_kernel(parts, codes, out):
    total = jnp.sum(parts[...].astype(F32), axis=0)
    groups = codes.shape[0]
    for within in range(4):
        keep = (lax.shift_right_logical(jnp.full(codes.shape, KEEP_BITS[within], jnp.int32), codes[...]) & 1) == 1
        rows = total[within * groups : (within + 1) * groups]
        out[pl.ds(within, groups, stride=4), :] = jnp.where(keep, rows, 0.0)


def doc_layout(lengths, row_total):
    doc_ends = jnp.cumsum(lengths, dtype=jnp.int32)
    positions = jnp.arange(row_total, dtype=jnp.int32)
    passed = positions[:, None] >= doc_ends[None, :]
    segment = jnp.sum(passed.astype(jnp.int32), axis=1, dtype=jnp.int32)
    begins = jnp.sum(jnp.where(passed, lengths[None, :], 0), axis=1, dtype=jnp.int32)
    return segment, positions - begins, segment < lengths.shape[0] - 1


def angles(doc_pos):
    exponent = jnp.arange(HEAD_DIM // 2, dtype=F32) * (2.0 / HEAD_DIM)
    phases = doc_pos.astype(F32)[:, None] * jnp.power(F32(ROPE_BASE), -exponent)
    cos, sin = jnp.cos(phases), jnp.sin(phases)
    return jnp.concatenate([cos, cos], axis=1), jnp.concatenate([-sin, sin], axis=1)


def call(kernel, out_shape, *args, at=None, mib=20, flops=None):
    specs = [pl.BlockSpec(memory_space=pltpu.VMEM)] * len(args)
    if at is not None:
        args, specs = (at,) + args, [pl.BlockSpec(memory_space=pltpu.SMEM)] + specs
    params = pltpu.CompilerParams(vmem_limit_bytes=mib * MIB)
    cost = flops and pl.CostEstimate(flops=flops, bytes_accessed=0, transcendentals=0)
    return pl.pallas_call(
        kernel, out_shape=out_shape, in_specs=specs, compiler_params=params, cost_estimate=cost
    )(*args)


def shape(dims, kind=BF16):
    return jax.ShapeDtypeStruct(dims, kind)


def shifted(value, axis, by):
    size = lax.axis_size(axis)
    return lax.ppermute(value, axis, [(i, (i + by) % size) for i in range(size)])


def copies(value, count):
    return jnp.broadcast_to(value[None], (count,) + value.shape)


def after(value, *earlier):
    return lax.optimization_barrier((value,) + earlier)[0]


def shards(hidden, target, qw, kw, vw, ow, qc, kc, vc, oc, doc_lengths):
    tokens = hidden.shape[0]
    n_z, n_y, n_c, n_x = (lax.axis_size(a) for a in ("zl", "y", "c", "x"))
    y_at, c_at, zh_at, x_at = (lax.axis_index(a) for a in ("y", "c", "zh", "x"))
    at = jnp.stack([y_at, zh_at, c_at])
    rows, q_width = qw.shape
    width = q_width + 2 * kw.shape[1]
    heads = q_width // HEAD_DIM
    depth = n_z * n_c * rows

    mine = call(compact_qkv_kernel, shape((n_z, 3 * rows // 4, width)), qw, kw, vw, qc, kc, vc, mib=58)
    w_own = lax.all_to_all(mine, "zl", 0, 0)

    split = call(split_hidden_kernel, [shape((tokens, depth))] * n_y, hidden, at=at, mib=40)
    slots = [split[0]] + [shifted(split[s], "y", s) for s in range(1, n_y)]
    segment, doc_pos, live = doc_layout(doc_lengths[0], tokens)
    cos, sin = angles(doc_pos)
    spot = jnp.arange(tokens)
    allow = (segment[:, None] == segment[None, :]) & (spot[None, :] <= spot[:, None])
    allow = allow.astype(F32)
    w_oth = shifted(w_own, "c", 1)
    w_own, w_oth, cos, sin, allow, *slots = lax.optimization_barrier((w_own, w_oth, cos, sin, allow, *slots))

    out_mine = call(mask_out_kernel, shape((ow.shape[1], ow.shape[0])), ow, oc)
    trade = []
    for z in range(n_z):
        for half in range(2):
            other = (z - 1 if half == 0 else z + 1) * 2 + 1 - half
            trade.append((z * 2 + half, other if z % 2 != half else z * 2 + half))
    out_mine = lax.ppermute(out_mine, ("zl", "zh"), trade)
    out_mine = after(out_mine, w_own)
    out_z = lax.all_to_all(copies(out_mine, n_z), "zl", 0, 0)

    terms = call(
        project_kernel,
        [shape((tokens, width), F32)] + [shape((tokens, width))] * (n_y - 1),
        w_own,
        w_oth,
        *slots,
    )
    terms = [terms[0]] + [shifted(terms[s], "y", -s) for s in range(1, n_y)]

    out_z = after(out_z, *terms).reshape(n_z // 2, 2, ow.shape[1], ow.shape[0])
    out_w = lax.all_gather(out_z, ("y", "c"), axis=0)

    queries, values, prob, att = call(
        attend_kernel,
        (
            shape((tokens, q_width)),
            shape((tokens, HEAD_DIM)),
            shape((heads, tokens, tokens), F32),
            shape((tokens, q_width)),
        ),
        *terms,
        cos,
        sin,
        allow,
        mib=58,
    )

    att_oth = shifted(att, "zh", 1)
    block = target.shape[1] // (n_x * 2)
    part = call(out_kernel, shape((n_x, tokens, block)), att, att_oth, out_w, at=at)
    blocks = lax.all_to_all(part, "x", 0, 0)
    target_share = lax.dynamic_slice_in_dim(target, (x_at * 2 + zh_at) * block, block, 1)
    block_out, error = call(
        error_kernel,
        (shape((tokens, block)), shape((n_x, tokens, block))),
        blocks,
        target_share,
        live[:, None].astype(F32),
    )
    errors = lax.all_to_all(error, "x", 0, 0)
    d_oth = call(functools.partial(d_att_kernel, 1), shape(att.shape), errors, out_w, at=at)
    d_oth = shifted(d_oth, "zh", 1)
    d_own = call(functools.partial(d_att_kernel, 0), shape(att.shape, F32), errors, out_w, at=at)

    d_key = call(
        key_grad_kernel, shape((n_y, tokens, HEAD_DIM)), d_own, d_oth, queries, values, prob, cos, sin
    )
    d_keys = lax.all_to_all(d_key, "y", 0, 0)
    half = (n_z, rows, HEAD_DIM)
    g_own, g_oth = call(grad_kernel, (shape(half, F32), shape(half)), *slots, d_keys, at=at)
    grad = (g_own + shifted(g_oth, "c", 1).astype(F32)).astype(BF16)
    grad = lax.all_to_all(grad, "zl", 0, 0)
    grad_key = call(final_kernel, shape((rows, HEAD_DIM), F32), grad, kc)
    return block_out, grad_key


def solution(mesh):
    fine = Mesh(mesh.devices.reshape(8, 4, 2, 4, 2), ("zl", "y", "c", "x", "zh"))
    dp, mp = ("zl", "y", "c"), ("x", "zh")
    by_dp, by_both, by_mp = P(dp, None), P(dp, mp), P(mp, dp)
    placed = (by_dp, by_dp) + (by_both,) * 3 + (by_mp,) + (by_both,) * 3 + (by_mp, by_dp)
    return jax.shard_map(
        shards, mesh=fine, in_specs=placed, out_specs=(by_both, by_both), check_vma=False
    )
```

```python
import functools

import jax
import jax.numpy as jnp
from jax import lax
from jax.experimental import pallas as pl
from jax.experimental.pallas import tpu as pltpu
from jax.sharding import Mesh, PartitionSpec as P

HEAD_DIM = 128
LOSS_DIV = 16
ROPE_BASE = 500000.0
KEEP_BITS = (0b000111, 0b011001, 0b101010, 0b110100)
MIB = 1024 * 1024
F32 = jnp.float32
BF16 = jnp.bfloat16
NT = (((1,), (1,)), ((), ()))
TN = (((0,), (0,)), ((), ()))


def keep_mask(codes, rows):
    groups = codes.shape[0]
    at_row = lax.broadcasted_iota(jnp.int32, (rows, groups), 0)
    at_group = lax.broadcasted_iota(jnp.int32, (rows, groups), 1)
    spread = jnp.where(at_row // 4 == at_group, 1.0, 0.0).astype(BF16)
    wide = jnp.dot(spread, codes.astype(F32).astype(BF16), preferred_element_type=F32)
    wide = wide.astype(jnp.int32)
    within = lax.broadcasted_iota(jnp.int32, wide.shape, 0) % 4
    bits = jnp.where(
        within == 0,
        KEEP_BITS[0],
        jnp.where(within == 1, KEEP_BITS[1], jnp.where(within == 2, KEEP_BITS[2], KEEP_BITS[3])),
    )
    return (lax.shift_right_logical(bits, wide) & 1) == 1


def masked(weight, codes):
    kept = jnp.where(keep_mask(codes, weight.shape[0]), weight.astype(F32), 0.0)
    return kept.astype(BF16)


def compact_qkv_kernel(qw, kw, vw, qc, kc, vc, out):
    weight = jnp.concatenate([qw[...], kw[...], vw[...]], axis=1)
    codes = jnp.concatenate([qc[...], kc[...], vc[...]], axis=1)
    groups, rows = codes.shape[0], weight.shape[0]
    at_group = lax.broadcasted_iota(jnp.int32, (groups, rows), 0)
    at_row = lax.broadcasted_iota(jnp.int32, (groups, rows), 1)
    plane = []
    for within in range(4):
        pick = jnp.where(at_row == 4 * at_group + within, 1.0, 0.0).astype(BF16)
        plane.append(jnp.dot(pick, weight, preferred_element_type=F32))
    first = jnp.where(codes < 3, plane[0], jnp.where(codes < 5, plane[1], plane[2]))
    second = jnp.where((codes == 1) | (codes == 3), plane[2], plane[3])
    second = jnp.where(codes == 0, plane[1], second)
    kept = jnp.concatenate([first, second, codes.astype(F32)], axis=0).astype(BF16)
    for copy in range(out.shape[0]):
        out[copy] = kept


def spread(kept):
    pieces, rows, width = kept.shape
    groups = rows // 3
    first, second, code = (
        kept[:, at * groups : (at + 1) * groups, :].astype(F32).reshape(pieces * groups, width)
        for at in range(3)
    )
    mid = (code == 3) | (code == 4)
    planes = (
        jnp.where(code < 3, first, 0.0),
        jnp.where(code == 0, second, jnp.where(mid, first, 0.0)),
        jnp.where((code == 1) | (code == 3), second, jnp.where(code == 5, first, 0.0)),
        jnp.where((code == 2) | (code > 3), second, 0.0),
    )
    return jnp.concatenate(planes, axis=0).astype(BF16)


def mask_out_kernel(ow, oc, out):
    kept = masked(ow[...], oc[...])
    cols = kept.shape[1]
    eye = lax.broadcasted_iota(jnp.int32, (cols, cols), 0) == lax.broadcasted_iota(
        jnp.int32, (cols, cols), 1
    )
    eye = jnp.where(eye, 1.0, 0.0).astype(BF16)
    out[...] = lax.dot_general(eye, kept, NT, preferred_element_type=F32).astype(BF16)


def split_hidden_kernel(at_ref, hidden, *outs):
    shifts = len(outs)
    depth = outs[0].shape[1]
    n_z = depth // 128
    row = lax.broadcasted_iota(jnp.int32, (depth, 1), 0)
    z, core, group, within = row // 128, row % 128 // 64, row % 64 // 4, row % 4
    place = jnp.where(core == at_ref[2], 0, depth // 2) + within * (depth // 8) + z * 16 + group
    column = lax.broadcasted_iota(jnp.int32, (depth, depth), 1)
    order = jnp.where(column == place, 1.0, 0.0).astype(BF16)
    for shift, out in enumerate(outs):
        y_to = lax.rem(at_ref[0] + shift, shifts)
        parts = []
        for z in range(n_z):
            lane = pl.multiple_of((z * shifts + y_to) * 128, 128)
            parts.append(hidden[:, pl.ds(lane, 128)])
        columns = jnp.concatenate(parts, axis=1)
        out[...] = jnp.dot(columns, order, preferred_element_type=F32).astype(BF16)


def rotate(values, cos, sin):
    return values * cos + pltpu.roll(values, HEAD_DIM // 2, 1) * sin


def project_kernel(w_own, w_oth, s0, s1, s2, s3, p0, p1, p2, p3):
    own, oth = spread(w_own), spread(w_oth)
    half = own.shape[0]
    for slot, term in ((s2, p2), (s1, p1), (s3, p3), (s0, p0)):
        total = jnp.dot(slot[:, :half], own, preferred_element_type=F32)
        total += jnp.dot(slot[:, half:], oth, preferred_element_type=F32)
        term[...] = total.astype(term.dtype)


def attend_kernel(p0, p1, p2, p3, cos, sin, allow, q_out, v_out, prob_out, att_out):
    raw = p0[...] + p1[...].astype(F32) + p2[...].astype(F32) + p3[...].astype(F32)
    heads = q_out.shape[1] // HEAD_DIM
    at = heads * HEAD_DIM
    keys = rotate(raw[:, at : at + HEAD_DIM], cos[...], sin[...]).astype(BF16)
    values = raw[:, at + HEAD_DIM :].astype(BF16)
    v_out[...] = values
    for head in range(heads):
        cut = slice(head * HEAD_DIM, (head + 1) * HEAD_DIM)
        query = rotate(raw[:, cut], cos[...], sin[...]).astype(BF16)
        q_out[:, cut] = query
        scores = lax.dot_general(query, keys, NT, preferred_element_type=F32)
        raised = jnp.where(allow[...] > 0.5, jnp.exp(scores * HEAD_DIM**-0.5), 0.0)
        prob = raised / jnp.sum(raised, axis=1, keepdims=True)
        prob_out[head] = prob
        att_out[:, cut] = jnp.dot(prob.astype(BF16), values, preferred_element_type=F32).astype(
            BF16
        )


def key_grad_kernel(d_own, d_other, q_ref, v_ref, prob_ref, cos, sin, out):
    d_att = (d_own[...] + d_other[...].astype(F32)).astype(BF16)
    total = jnp.zeros(out.shape[1:], F32)
    for head in range(prob_ref.shape[0]):
        cut = slice(head * HEAD_DIM, (head + 1) * HEAD_DIM)
        d_prob = lax.dot_general(d_att[:, cut], v_ref[...], NT, preferred_element_type=F32)
        prob = prob_ref[head]
        row_dot = jnp.sum(prob * d_prob, axis=1, keepdims=True)
        d_score = (prob * (d_prob - row_dot) * HEAD_DIM**-0.5).astype(BF16)
        total += lax.dot_general(d_score, q_ref[:, cut], TN, preferred_element_type=F32)
    d_key = rotate(total, cos[...], -sin[...]).astype(BF16)
    for copy in range(out.shape[0]):
        out[copy] = d_key


def out_block(weight, k, r):
    return jnp.concatenate([weight[part, k, r] for part in range(weight.shape[0])], axis=0)


def out_kernel(at_ref, own, oth, weight, out):
    zh = at_ref[1]
    for k in range(out.shape[0]):
        total = lax.dot_general(own[...], out_block(weight, k, zh), NT, preferred_element_type=F32)
        total += lax.dot_general(oth[...], out_block(weight, k, 1 - zh), NT, preferred_element_type=F32)
        out[k] = total.astype(out.dtype)


def d_att_kernel(which, at_ref, errors, weight, out):
    r = at_ref[1] if which == 0 else 1 - at_ref[1]
    total = jnp.zeros(out.shape, F32)
    for k in range(errors.shape[0]):
        total += jnp.dot(errors[k], out_block(weight, k, r), preferred_element_type=F32)
    out[...] = total.astype(out.dtype)


def error_kernel(blocks, target, live, block_out, errors):
    total = jnp.sum(blocks[...].astype(F32), axis=0)
    block_out[...] = total.astype(BF16)
    error = ((total - target[...].astype(F32)) * live[...] / LOSS_DIV).astype(BF16)
    for k in range(errors.shape[0]):
        errors[k] = error


def grad_kernel(at_ref, s0, s1, s2, s3, d_keys, own, oth):
    pieces, rows = own.shape[:2]
    half, groups = pieces * rows, rows // 4
    n_y = d_keys.shape[0]
    for at, out in ((half, oth), (0, own)):
        total = jnp.zeros((half, out.shape[2]), F32)
        for shift, slot in enumerate((s0, s1, s2, s3)):
            d_key = d_keys[lax.rem(at_ref[0] + n_y - shift, n_y)]
            total += lax.dot_general(slot[:, at : at + half], d_key, TN, preferred_element_type=F32)
        total = total.astype(out.dtype)
        for within in range(4):
            for z in range(pieces):
                start = (within * pieces + z) * groups
                out[z, within * groups : (within + 1) * groups] = total[start : start + groups]


def final_kernel(parts, codes, out):
    total = jnp.sum(parts[...].astype(F32), axis=0)
    groups = codes.shape[0]
    for within in range(4):
        keep = (lax.shift_right_logical(jnp.full(codes.shape, KEEP_BITS[within], jnp.int32), codes[...]) & 1) == 1
        rows = total[within * groups : (within + 1) * groups]
        out[pl.ds(within, groups, stride=4), :] = jnp.where(keep, rows, 0.0)


def doc_layout(lengths, row_total):
    doc_ends = jnp.cumsum(lengths, dtype=jnp.int32)
    positions = jnp.arange(row_total, dtype=jnp.int32)
    passed = positions[:, None] >= doc_ends[None, :]
    segment = jnp.sum(passed.astype(jnp.int32), axis=1, dtype=jnp.int32)
    begins = jnp.sum(jnp.where(passed, lengths[None, :], 0), axis=1, dtype=jnp.int32)
    return segment, positions - begins, segment < lengths.shape[0] - 1


def angles(doc_pos):
    exponent = jnp.arange(HEAD_DIM // 2, dtype=F32) * (2.0 / HEAD_DIM)
    phases = doc_pos.astype(F32)[:, None] * jnp.power(F32(ROPE_BASE), -exponent)
    cos, sin = jnp.cos(phases), jnp.sin(phases)
    return jnp.concatenate([cos, cos], axis=1), jnp.concatenate([-sin, sin], axis=1)


def call(kernel, out_shape, *args, at=None, mib=20, flops=None):
    specs = [pl.BlockSpec(memory_space=pltpu.VMEM)] * len(args)
    if at is not None:
        args, specs = (at,) + args, [pl.BlockSpec(memory_space=pltpu.SMEM)] + specs
    params = pltpu.CompilerParams(vmem_limit_bytes=mib * MIB)
    cost = flops and pl.CostEstimate(flops=flops, bytes_accessed=0, transcendentals=0)
    return pl.pallas_call(
        kernel, out_shape=out_shape, in_specs=specs, compiler_params=params, cost_estimate=cost
    )(*args)


def shape(dims, kind=BF16):
    return jax.ShapeDtypeStruct(dims, kind)


def shifted(value, axis, by):
    size = lax.axis_size(axis)
    return lax.ppermute(value, axis, [(i, (i + by) % size) for i in range(size)])


def copies(value, count):
    return jnp.broadcast_to(value[None], (count,) + value.shape)


def after(value, *earlier):
    return lax.optimization_barrier((value,) + earlier)[0]


def shards(hidden, target, qw, kw, vw, ow, qc, kc, vc, oc, doc_lengths):
    tokens = hidden.shape[0]
    n_z, n_y, n_c, n_x = (lax.axis_size(a) for a in ("zl", "y", "c", "x"))
    y_at, c_at, zh_at, x_at = (lax.axis_index(a) for a in ("y", "c", "zh", "x"))
    at = jnp.stack([y_at, zh_at, c_at])
    rows, q_width = qw.shape
    width = q_width + 2 * kw.shape[1]
    heads = q_width // HEAD_DIM
    depth = n_z * n_c * rows

    mine = call(compact_qkv_kernel, shape((n_z, 3 * rows // 4, width)), qw, kw, vw, qc, kc, vc, mib=58)
    w_own = lax.all_to_all(mine, "zl", 0, 0)

    split = call(split_hidden_kernel, [shape((tokens, depth))] * n_y, hidden, at=at, mib=40)
    slots = [split[0]] + [shifted(split[s], "y", s) for s in range(1, n_y)]
    segment, doc_pos, live = doc_layout(doc_lengths[0], tokens)
    cos, sin = angles(doc_pos)
    spot = jnp.arange(tokens)
    allow = (segment[:, None] == segment[None, :]) & (spot[None, :] <= spot[:, None])
    allow = allow.astype(F32)
    w_oth = shifted(w_own, "c", 1)
    w_own, w_oth, cos, sin, allow, *slots = lax.optimization_barrier((w_own, w_oth, cos, sin, allow, *slots))

    out_mine = call(mask_out_kernel, shape((ow.shape[1], ow.shape[0])), ow, oc)
    trade = []
    for z in range(n_z):
        for half in range(2):
            other = (z - 1 if half == 0 else z + 1) * 2 + 1 - half
            trade.append((z * 2 + half, other if z % 2 != half else z * 2 + half))
    out_mine = lax.ppermute(out_mine, ("zl", "zh"), trade)
    out_mine = after(out_mine, w_own)
    out_z = lax.all_to_all(copies(out_mine, n_z), "zl", 0, 0)

    terms = call(
        project_kernel,
        [shape((tokens, width), F32)] + [shape((tokens, width))] * (n_y - 1),
        w_own,
        w_oth,
        *slots,
    )
    terms = [terms[0]] + [shifted(terms[s], "y", -s) for s in range(1, n_y)]

    out_z = after(out_z, terms[1]).reshape(n_z // 2, 2, ow.shape[1], ow.shape[0])
    out_w = lax.all_gather(out_z, ("y", "c"), axis=0)

    queries, values, prob, att = call(
        attend_kernel,
        (
            shape((tokens, q_width)),
            shape((tokens, HEAD_DIM)),
            shape((heads, tokens, tokens), F32),
            shape((tokens, q_width)),
        ),
        *terms,
        cos,
        sin,
        allow,
        mib=58,
        flops=10**11,
    )

    att_oth = shifted(att, "zh", 1)
    block = target.shape[1] // (n_x * 2)
    part = call(out_kernel, shape((n_x, tokens, block)), att, att_oth, out_w, at=at)
    blocks = lax.all_to_all(part, "x", 0, 0)
    target_share = lax.dynamic_slice_in_dim(target, (x_at * 2 + zh_at) * block, block, 1)
    block_out, error = call(
        error_kernel,
        (shape((tokens, block)), shape((n_x, tokens, block))),
        blocks,
        target_share,
        live[:, None].astype(F32),
    )
    errors = lax.all_to_all(error, "x", 0, 0)
    d_oth = call(functools.partial(d_att_kernel, 1), shape(att.shape), errors, out_w, at=at)
    d_oth = shifted(d_oth, "zh", 1)
    d_own = call(functools.partial(d_att_kernel, 0), shape(att.shape, F32), errors, out_w, at=at)

    d_key = call(
        key_grad_kernel, shape((n_y, tokens, HEAD_DIM)), d_own, d_oth, queries, values, prob, cos, sin
    )
    d_keys = lax.all_to_all(d_key, "y", 0, 0)
    half = (n_z, rows, HEAD_DIM)
    g_own, g_oth = call(grad_kernel, (shape(half, F32), shape(half)), *slots, d_keys, at=at)
    grad = (g_own + shifted(g_oth, "c", 1).astype(F32)).astype(BF16)
    grad = lax.all_to_all(grad, "zl", 0, 0)
    grad_key = call(final_kernel, shape((rows, HEAD_DIM), F32), grad, kc)
    return block_out, grad_key


def solution(mesh):
    fine = Mesh(mesh.devices.reshape(8, 4, 2, 4, 2), ("zl", "y", "c", "x", "zh"))
    dp, mp = ("zl", "y", "c"), ("x", "zh")
    by_dp, by_both, by_mp = P(dp, None), P(dp, mp), P(mp, dp)
    placed = (by_dp, by_dp) + (by_both,) * 3 + (by_mp,) + (by_both,) * 3 + (by_mp, by_dp)
    return jax.shard_map(
        shards, mesh=fine, in_specs=placed, out_specs=(by_both, by_both), check_vma=False
    )
```
